32 devices in a mesh: seq: 16 (over z, y, core), head: 2 (over x), dp: 1.
Axes of the slice: x: 2, y: 2, z: 4, core: 2. Of those that a mesh axis runs over, the one named last changes fastest.
Arguments:
- queries: bfloat16 [4096, 2048], P(('dp', 'seq', 'head')), may hold values from -9 to 9
- keys: bfloat16 [4096, 2048], P(('dp', 'seq', 'head')), may hold values from -9 to 9
- values: bfloat16 [4096, 2048], P(('dp', 'seq', 'head')), may hold values from -6 to 6
- coords: int32 [3, 4096], P(None, ('dp', 'seq', 'head')), may hold values from 0 to 511, as said below
- lengths: int32 [32], P('dp'), may hold values from 1 to 384, 4096 in all
Outputs:
- attention: bfloat16 [4096, 2048], P(('dp', 'seq', 'head'))
The draws below stay inside these ranges and needn't reach their ends.
Inputs may be any that keep to these rules, and one draw needn't show every extreme that they name: `coords`: voxel coordinates of each token along x, y and z. `lengths`: the token counts of the 32 scenes of a pack in order; they sum to 4096 and the longest scene has exactly 384 tokens.
All inputs are finite; a program needn't handle non-finite values.
Results may differ from the reference program's by a relative error of at most 0.012.
Values may be sent and summed in bfloat16 or wider, within the bound.
A program may use at most 128 MiB of HBM per device.

```python
import math
import jax
import jax.numpy as jnp
import numpy as np
from jax import lax

H = 32
HD = 64
SCENES = 32
GROUP = 256
TOKENS = 4096
MOST = 384
REACH = 2


def make_coords(key):
    return jax.random.randint(jax.random.fold_in(key, 11), (3, TOKENS), 0, 512).astype(jnp.int32)


def drawn_draw(key):
    return jnp.clip(jax.random.normal(key, (TOKENS, H * HD), jnp.float32), -6.0, 6.0)


def draw_coords(key, part):
    return make_coords(key)


def draw_queries(key, part):
    drawn = drawn_draw(jax.random.fold_in(key, 31))
    return drawn.astype(jnp.bfloat16)


def draw_keys(key, part):
    drawn = drawn_draw(jax.random.fold_in(key, 37))
    return drawn.astype(jnp.bfloat16)


def level_of(own_key, shape, shards, smallest, high):
    def one(dim, blocks):
        steps = jax.random.uniform(jax.random.fold_in(jax.random.fold_in(own_key, 6), dim), (blocks,), jnp.float32, smallest / len(shards), high / len(shards))
        return jnp.repeat(jnp.exp(steps), shape[dim] // blocks).reshape((-1,) + (1,) * (len(shape) - dim - 1))

    loudness = one(*shards[0])
    for cut in shards[1:]:
        loudness = loudness * one(*cut)
    return loudness


def length_profile(number_of, total, limit, slope):
    portions = [(1 << 20) // math.isqrt(rank ** slope) + 1 for rank in range(2, number_of + 1)]
    rest, counts = total - limit - (number_of - 1), [1] * (number_of - 1)
    while rest > 0:
        candidates = [i for i in range(number_of - 1) if counts[i] < limit]
        whole, left = sum([portions[i] for i in candidates]), rest
        for i in candidates:
            extra = min(limit - counts[i], max(1, left * portions[i] // whole), rest)
            counts[i] = counts[i] + extra
            rest = rest - extra
    return np.array([limit] + counts)


def ragged_sizes(rng, number_of, total, limit, lean):
    if number_of == 2:
        one = jax.random.randint(rng, (), max(1, total - limit), min(limit, total - 1) + 1)
        return jnp.stack([one, total - one])
    sizes = jnp.asarray(length_profile(number_of, total, limit, lean), jnp.int32)
    couples = (number_of - 1) // 2
    giver, sink = sizes[1:1 + 2 * couples:2], sizes[2:2 + 2 * couples:2]
    room = jnp.minimum(giver - 1, limit - sink)
    passed = jax.random.randint(jax.random.fold_in(rng, 1), (couples,), 0, 1 << 20) % (room + 1)
    sizes = sizes.at[1:1 + 2 * couples:2].set(giver - passed).at[2:2 + 2 * couples:2].set(sink + passed)
    return sizes[jax.random.permutation(jax.random.fold_in(rng, 2), number_of)]


def normal_values(rng, dims, deviation, limit, split=(), kind=jnp.bfloat16):
    values = deviation * jax.random.normal(rng, dims, jnp.float32)
    if split:
        values = values * level_of(rng, dims, split, -0.22, 0.18)
    return jnp.clip(values, -limit, limit).astype(kind)


def setup_inputs(seed: int = 0, part: int = 0) -> dict:
    key_list = jax.random.split(jax.random.key(seed), 6)
    part_splits = jax.random.split(jax.random.fold_in(key_list[5], part), 6)
    return {
        "queries": draw_queries(jax.random.fold_in(jax.random.fold_in(key_list[5], part), 71), part),
        "keys": draw_keys(jax.random.fold_in(jax.random.fold_in(key_list[5], part), 71), part),
        "values": normal_values(part_splits[2], (TOKENS, H * HD), 1.0, 6.0, ((0, 32),)),
        "coords": draw_coords(jax.random.fold_in(jax.random.fold_in(key_list[5], part), 71), part),
        "lengths": ragged_sizes(part_splits[4], SCENES, TOKENS, MOST, 2).astype(jnp.int32),
    }


score_scale = 0.125
neg_big = -1.0e30


def rotary_angles(coords):
    pair_count = HD // 2
    pair_id = jnp.arange(pair_count, dtype=jnp.int32)
    axis_of = (3 * pair_id) // pair_count
    exponent = ((3 * pair_id) % pair_count).astype(jnp.float32) / pair_count
    frequency = jnp.power(jnp.float32(100.0), -exponent)
    position = coords.astype(jnp.float32)
    angles = jnp.zeros((coords.shape[1], pair_count), jnp.float32)
    for axis_id in range(3):
        picked = jnp.where(axis_of == axis_id, frequency, jnp.float32(0.0))
        angles = angles + position[axis_id][:, None] * picked[None, :]
    return angles


def rotate_rows(source, angles):
    row_count = source.shape[0]
    per_head = source.reshape(row_count, -1, HD).astype(jnp.float32)
    half_size = HD // 2
    front_half = per_head[..., :half_size]
    back_half = per_head[..., half_size:]
    cos_val = jnp.cos(angles)[:, None, :]
    sin_val = jnp.sin(angles)[:, None, :]
    turned = jnp.concatenate([front_half * cos_val - back_half * sin_val, front_half * sin_val + back_half * cos_val], axis=-1)
    return turned.reshape(row_count, -1)


def scene_of(positions, lengths):
    scene_end = jnp.cumsum(lengths).astype(jnp.int32)
    return jnp.sum((positions[:, None] >= scene_end[None, :]).astype(jnp.int32), axis=1).astype(jnp.int32)


def reference(queries, keys, values, coords, lengths):
    angles = rotary_angles(coords)
    q_heads = rotate_rows(queries, angles).astype(jnp.bfloat16).reshape(TOKENS, H, HD).transpose(1, 0, 2)
    k_heads = rotate_rows(keys, angles).astype(jnp.bfloat16).reshape(TOKENS, H, HD).transpose(1, 0, 2)
    v_heads = values.reshape(TOKENS, H, HD).transpose(1, 0, 2)
    scene = scene_of(jnp.arange(TOKENS, dtype=jnp.int32), lengths)
    margin = REACH * GROUP
    window = (2 * REACH + 1) * GROUP
    scene_pad = jnp.pad(scene, (margin, margin), constant_values=-1).astype(jnp.int32)
    block_starts = (jnp.arange(TOKENS // GROUP, dtype=jnp.int32) * GROUP).astype(jnp.int32)

    def one_head(operands):
        q_one, k_one, v_one = operands
        k_pad = jnp.pad(k_one, ((margin, margin), (0, 0)))
        v_pad = jnp.pad(v_one, ((margin, margin), (0, 0)))

        def one_block(block_start):
            query_block = lax.dynamic_slice_in_dim(q_one, block_start, GROUP, 0)
            query_scene = lax.dynamic_slice_in_dim(scene, block_start, GROUP, 0)
            key_block = lax.dynamic_slice_in_dim(k_pad, block_start, window, 0)
            value_block = lax.dynamic_slice_in_dim(v_pad, block_start, window, 0)
            key_scene = lax.dynamic_slice_in_dim(scene_pad, block_start, window, 0)
            scores = jnp.dot(query_block, key_block.T, preferred_element_type=jnp.float32) * score_scale
            allowed = query_scene[:, None] == key_scene[None, :]
            row_top = jnp.max(jnp.where(allowed, scores, neg_big), axis=1, keepdims=True)
            raw_weights = jnp.where(allowed, jnp.exp(scores - row_top), jnp.float32(0.0))
            weight_sum = jnp.sum(raw_weights, axis=1, keepdims=True)
            mixed = jnp.dot(raw_weights.astype(jnp.bfloat16), value_block, preferred_element_type=jnp.float32)
            return mixed / weight_sum

        return lax.map(one_block, block_starts).reshape(TOKENS, HD)

    result = lax.map(one_head, (q_heads, k_heads, v_heads))
    return result.transpose(1, 0, 2).reshape(TOKENS, H * HD).astype(jnp.bfloat16)
```

```python
import functools

import jax
import jax.numpy as jnp
import numpy as np
from jax import lax
from jax.experimental import pallas as pl
from jax.experimental.pallas import tpu as pltpu
from jax.sharding import PartitionSpec as P

HD = 64
GROUP_DEVICES = 8
NEG_BIG = -1e30
SCORE_SCALE = 0.125


def frequency_rows():
    pair_count = HD // 2
    pair = np.arange(pair_count)
    exponent = (3 * pair % pair_count) / pair_count
    column = (100.0 ** -exponent).astype(np.float32)
    return np.tile(column[:, None], (1, 128))


def attention_kernel(
    sizes,
    q_hbm, k_hbm, v_hbm, coords_ref, lengths_ref, freq_ref,
    out_ref,
    q_in, k_in, q_rot, k_rot, q_buf, k_buf, v_buf, o_buf, key_scene, query_scene,
    in_sem, q_send, q_recv, kv_send, kv_recv, halo_send, o_send, o_recv, own_sem,
):
    head_count, members, groups, rows, cols, reach_blocks, scenes = sizes
    heads = cols // HD
    spans = -(-reach_blocks // members)
    blocks = members + 2 * reach_blocks
    window = (2 * reach_blocks + 1) * rows
    flat = lax.axis_index("seq") * head_count + lax.axis_index("head")
    group = flat // members
    me = flat % members

    def device(group_at, member_at):
        at = group_at * members + member_at
        return {"seq": at // head_count, "head": at % head_count}

    def columns(member_at):
        return pl.ds(pl.multiple_of(member_at * cols, cols), cols)

    def block(index):
        return pl.ds(pl.multiple_of(index * rows, rows), rows)

    shifts = [e for d in range(1, spans + 1) for e in (d, -d)]

    load_k = pltpu.make_async_copy(k_hbm, k_in, in_sem.at[0])
    load_q = pltpu.make_async_copy(q_hbm, q_in, in_sem.at[1])
    load_k.start()
    load_q.start()
    own_v = pltpu.make_async_copy(
        v_hbm.at[:, columns(me)], v_buf.at[block(reach_blocks + me)], own_sem.at[0]
    )
    own_v.start()

    barrier = pltpu.get_barrier_semaphore()
    for i in range(1, members):
        pl.semaphore_signal(barrier, inc=1, device_id=device(group, (me + i) % members))
    expected = members - 1
    for e in shifts:
        there = (group + e >= 0) & (group + e < groups)

        @pl.when(there)
        def _():
            pl.semaphore_signal(barrier, inc=1, device_id=device(group + e, me))

        expected = expected + there.astype(jnp.int32)
    pl.semaphore_wait(barrier, expected)

    bufs = (v_buf, k_buf)

    def kv_copy(which, source, i, other, index):
        return pltpu.make_async_remote_copy(
            src_ref=source,
            dst_ref=bufs[which].at[block(index)],
            send_sem=kv_send.at[which, i],
            recv_sem=kv_recv.at[which, index],
            device_id=device(group, other),
        )

    v_copies = []
    for i in range(1, members):
        other = (me + i) % members
        copy = kv_copy(0, v_hbm.at[:, columns(other)], i, other, reach_blocks + me)
        copy.start()
        v_copies.append(copy)

    pair = lax.broadcasted_iota(jnp.int32, (HD // 2, rows), 0)
    axis_of = 3 * pair // (HD // 2)
    position = jnp.where(
        axis_of == 0,
        coords_ref[0:1, :],
        jnp.where(axis_of == 1, coords_ref[1:2, :], coords_ref[2:3, :]),
    ).astype(jnp.float32)
    angles = position * freq_ref[...]

    def spread(table):
        tall = jnp.concatenate([table] * (128 // (HD // 2)), axis=0).T
        return jnp.concatenate([tall] * (cols // 128), axis=1)

    cos_all = spread(jnp.cos(angles))
    sin_all = spread(jnp.sin(angles))
    from_row = lax.broadcasted_iota(jnp.int32, (cols, cols), 0)
    to_col = lax.broadcasted_iota(jnp.int32, (cols, cols), 1)
    front = to_col % HD < HD // 2
    swap = jnp.where(
        front & (from_row == to_col + HD // 2),
        -1.0,
        jnp.where((to_col % HD >= HD // 2) & (from_row == to_col - HD // 2), 1.0, 0.0),
    ).astype(jnp.bfloat16)

    def rotated(tile, scale):
        swapped = jnp.dot(tile, swap, preferred_element_type=jnp.float32)
        turned = tile.astype(jnp.float32) * cos_all + swapped * sin_all
        return (turned * scale).astype(jnp.bfloat16)

    load_k.wait()
    k_copies = []
    for i in range(1, members):
        other = (me + i) % members
        k_rot[i] = rotated(k_in[:, columns(other)], 1.0)
        copy = kv_copy(1, k_rot.at[i], i, other, reach_blocks + me)
        copy.start()
        k_copies.append(copy)
    k_buf[block(reach_blocks + me), :] = rotated(k_in[:, columns(me)], 1.0)

    load_q.wait()
    q_copies = []
    for i in range(1, members):
        other = (me + i) % members
        q_rot[i] = rotated(q_in[:, columns(other)], SCORE_SCALE)
        copy = pltpu.make_async_remote_copy(
            src_ref=q_rot.at[i],
            dst_ref=q_buf.at[block(me)],
            send_sem=q_send.at[i],
            recv_sem=q_recv.at[me],
            device_id=device(group, other),
        )
        copy.start()
        q_copies.append(copy)
    q_buf[block(me), :] = rotated(q_in[:, columns(me)], SCORE_SCALE)

    first = (group * members - reach_blocks) * rows
    token = first + lax.broadcasted_iota(jnp.int32, (8, blocks * rows), 1)
    scene = jnp.zeros((8, blocks * rows), jnp.int32)
    end = jnp.int32(0)
    for s in range(scenes):
        end = end + lengths_ref[s]
        scene = scene + (token >= end).astype(jnp.int32)
    key_scene[...] = jnp.where(token < 0, -1, scene).astype(jnp.float32)
    for b in range(members):
        row = key_scene[0:1, (reach_blocks + b) * rows : (reach_blocks + b + 1) * rows]
        query_scene[b] = jnp.broadcast_to(row, (128, rows)).T

    for e in shifts:
        held = [p for p in range(members) if 0 <= reach_blocks + p - e * members < blocks]
        low = (reach_blocks + held[0] - e * members) * rows
        high = (reach_blocks + held[-1] - e * members + 1) * rows

        @pl.when((group - e < 0) | (group - e >= groups))
        def _():
            for buf in bufs:
                buf[low:high, :] = jnp.zeros((high - low, cols), jnp.bfloat16)

    def halo_copy(which, p, e):
        index = reach_blocks + p - e * members
        return pltpu.make_async_remote_copy(
            src_ref=bufs[which].at[block(reach_blocks + p)],
            dst_ref=bufs[which].at[block(index)],
            send_sem=halo_send.at[which, shifts.index(e), p],
            recv_sem=kv_recv.at[which, index],
            device_id=device(group + e, me),
        )

    routes = [
        (p, [e for e in shifts if 0 <= reach_blocks + p - e * members < blocks])
        for p in range(members)
    ]
    routes.sort(key=lambda route: -len(route[1]))
    own_v.wait()
    for which in range(2):
        for p, goes in routes:

            @pl.when(me != p)
            def _():
                kv_copy(which, k_rot.at[0], 0, p, reach_blocks + p).wait_recv()

            for e in goes:

                @pl.when((group + e >= 0) & (group + e < groups))
                def _():
                    halo_copy(which, p, e).start()

    for which in range(2):
        for p, goes in routes:
            for e in goes:

                @pl.when((group - e >= 0) & (group - e < groups))
                def _():
                    halo_copy(which, p, e).wait_recv()

    for i in range(1, members):
        other = (me + i) % members
        pltpu.make_async_remote_copy(
            src_ref=q_rot.at[0],
            dst_ref=q_buf.at[block(other)],
            send_sem=q_send.at[0],
            recv_sem=q_recv.at[other],
            device_id=device(group, other),
        ).wait_recv()

    lane_head = lax.broadcasted_iota(jnp.int32, (rows, cols), 1) // HD

    def out_copy(i, other):
        return pltpu.make_async_remote_copy(
            src_ref=o_buf.at[i],
            dst_ref=out_ref.at[:, columns(me)],
            send_sem=o_send.at[i],
            recv_sem=o_recv.at[me],
            device_id=device(group, other),
        )

    def attend(i, carry):
        b = (me + i) % members
        q_tile = q_buf[block(b), :]
        span = pl.ds(pl.multiple_of(b * rows, rows), window)
        k_tile = k_buf[span, :]
        v_tile = v_buf[span, :]
        q_scene = jnp.concatenate([query_scene[b]] * (window // 128), axis=1)
        allowed = q_scene == key_scene[0:1, span]
        result = jnp.zeros((rows, cols), jnp.float32)
        for h in range(heads):
            q_one = jnp.where(lane_head == h, q_tile, jnp.bfloat16(0.0))
            scores = lax.dot_general(
                q_one, k_tile, (((1,), (1,)), ((), ())), preferred_element_type=jnp.float32
            )
            scores = jnp.where(allowed, scores, NEG_BIG)
            top = jnp.max(scores, axis=1, keepdims=True)
            weights = jnp.exp(scores - top)
            total = jnp.sum(weights, axis=1, keepdims=True)
            mixed = jnp.dot(
                weights.astype(jnp.bfloat16), v_tile, preferred_element_type=jnp.float32
            )
            result = jnp.where(lane_head == h, mixed / total, result)
        o_buf[i] = result.astype(jnp.bfloat16)
        return carry

    def attend_and_send(i, carry):
        attend(i, 0)
        out_copy(i, (me + i) % members).start()
        return carry

    lax.fori_loop(1, members, attend_and_send, 0)
    attend(0, 0)
    own_o = pltpu.make_async_copy(o_buf.at[0], out_ref.at[:, columns(me)], own_sem.at[1])
    own_o.start()

    for copy in v_copies + k_copies + q_copies:
        copy.wait_send()
    for which in range(2):
        for p, goes in routes:
            for e in goes:

                @pl.when((group + e >= 0) & (group + e < groups))
                def _():
                    halo_copy(which, p, e).wait_send()

    for i in range(1, members):
        out_copy(i, (me + i) % members).wait_send()
    for i in range(1, members):
        other = (me + i) % members
        pltpu.make_async_remote_copy(
            src_ref=o_buf.at[0],
            dst_ref=out_ref.at[:, columns(other)],
            send_sem=o_send.at[0],
            recv_sem=o_recv.at[other],
            device_id=device(group, other),
        ).wait_recv()
    own_o.wait()


def local(queries, keys, values, coords, lengths):
    rows, all_cols = queries.shape
    head_count = lax.axis_size("head")
    seq_count = lax.axis_size("seq")
    members = GROUP_DEVICES
    groups = seq_count * head_count // members
    cols = all_cols // members
    scenes = lengths.shape[0]
    total = rows * seq_count * head_count
    longest = 3 * total // scenes
    reach_blocks = -(-(longest - 1) // rows)
    blocks = members + 2 * reach_blocks
    spans = -(-reach_blocks // members)
    sizes = (head_count, members, groups, rows, cols, reach_blocks, scenes)
    window = (2 * reach_blocks + 1) * rows
    bf16, dma = jnp.bfloat16, pltpu.SemaphoreType.DMA
    anywhere = pl.BlockSpec(memory_space=pl.ANY)
    in_vmem = pl.BlockSpec(memory_space=pltpu.VMEM)
    return pl.pallas_call(
        functools.partial(attention_kernel, sizes),
        out_shape=jax.ShapeDtypeStruct((rows, all_cols), bf16),
        in_specs=[
            anywhere, anywhere, anywhere, in_vmem,
            pl.BlockSpec(memory_space=pltpu.SMEM), in_vmem,
        ],
        out_specs=anywhere,
        scratch_shapes=[
            pltpu.VMEM((rows, all_cols), bf16),
            pltpu.VMEM((rows, all_cols), bf16),
            pltpu.VMEM((members, rows, cols), bf16),
            pltpu.VMEM((members, rows, cols), bf16),
            pltpu.VMEM((members * rows, cols), bf16),
            pltpu.VMEM((blocks * rows, cols), bf16),
            pltpu.VMEM((blocks * rows, cols), bf16),
            pltpu.VMEM((members, rows, cols), bf16),
            pltpu.VMEM((8, blocks * rows), jnp.float32),
            pltpu.VMEM((members, rows, 128), jnp.float32),
            dma((2,)),
            dma((members,)),
            dma((members,)),
            dma((2, members)),
            dma((2, blocks)),
            dma((2, 2 * spans, members)),
            dma((members,)),
            dma((members,)),
            dma((2,)),
        ],
        compiler_params=pltpu.CompilerParams(
            collective_id=0, has_side_effects=True, vmem_limit_bytes=48 * 1024 * 1024
        ),
        cost_estimate=pl.CostEstimate(
            flops=4 * members * rows * window * cols,
            bytes_accessed=8 * rows * all_cols,
            transcendentals=members * rows * window * (cols // HD),
        ),
    )(queries, keys, values, coords, lengths, jnp.asarray(frequency_rows()))


def solution(mesh):
    in_specs = (
        P(("dp", "seq", "head"), None),
        P(("dp", "seq", "head"), None),
        P(("dp", "seq", "head"), None),
        P(None, ("dp", "seq", "head")),
        P("dp"),
    )
    out_specs = P(("dp", "seq", "head"), None)
    return jax.shard_map(local, mesh=mesh, in_specs=in_specs, out_specs=out_specs, check_vma=False)
```

```python
import functools

import jax
import jax.numpy as jnp
import numpy as np
from jax import lax
from jax.experimental import pallas as pl
from jax.experimental.pallas import tpu as pltpu
from jax.sharding import PartitionSpec as P

HD = 64
GROUP_DEVICES = 8
NEG_BIG = -1e30
SCORE_SCALE = 0.125


def frequencies():
    pair_count = HD // 2
    exponent = (3 * np.arange(pair_count) % pair_count) / pair_count
    return [float(f) for f in (100.0 ** -exponent).astype(np.float32)]


def attention_kernel(
    sizes,
    q_hbm, k_hbm, v_hbm, coords_hbm, lengths_hbm,
    out_ref,
    coords_ref, lengths_ref, q_in, k_in, q_rot, k_rot, q_buf, k_buf, v_buf, o_buf, key_scene, query_scene,
    in_sem, q_send, q_recv, kv_send, kv_recv, halo_send, o_send, o_recv, own_sem,
):
    head_count, members, groups, rows, cols, reach_blocks, scenes = sizes
    heads = cols // HD
    spans = -(-reach_blocks // members)
    blocks = members + 2 * reach_blocks
    window = (2 * reach_blocks + 1) * rows
    flat = lax.axis_index("seq") * head_count + lax.axis_index("head")
    group = flat // members
    me = flat % members

    def device(group_at, member_at):
        at = group_at * members + member_at
        return {"seq": at // head_count, "head": at % head_count}

    def columns(member_at):
        return pl.ds(pl.multiple_of(member_at * cols, cols), cols)

    def block(index):
        return pl.ds(pl.multiple_of(index * rows, rows), rows)

    shifts = [e for d in range(1, spans + 1) for e in (d, -d)]

    load_k = pltpu.make_async_copy(k_hbm, k_in, in_sem.at[0])
    load_q = pltpu.make_async_copy(q_hbm, q_in, in_sem.at[1])
    load_coords = pltpu.make_async_copy(coords_hbm, coords_ref, in_sem.at[2])
    load_lengths = pltpu.make_async_copy(lengths_hbm, lengths_ref, in_sem.at[3])
    load_coords.start()
    load_k.start()
    load_q.start()
    load_lengths.start()
    own_v = pltpu.make_async_copy(
        v_hbm.at[:, columns(me)], v_buf.at[reach_blocks + me], own_sem.at[0]
    )
    own_v.start()

    barrier = pltpu.get_barrier_semaphore()
    for i in range(1, members):
        pl.semaphore_signal(barrier, inc=1, device_id=device(group, (me + i) % members))
    expected = members - 1
    for e in shifts:
        there = (group + e >= 0) & (group + e < groups)

        @pl.when(there)
        def _():
            pl.semaphore_signal(barrier, inc=1, device_id=device(group + e, me))

        expected = expected + there.astype(jnp.int32)
    pl.semaphore_wait(barrier, expected)

    bufs = (v_buf, k_buf)

    def kv_copy(which, source, i, other, index):
        return pltpu.make_async_remote_copy(
            src_ref=source,
            dst_ref=bufs[which].at[index],
            send_sem=kv_send.at[which, i],
            recv_sem=kv_recv.at[which, index],
            device_id=device(group, other),
        )

    v_copies = []
    for i in range(1, members):
        other = (me + i) % members
        copy = kv_copy(0, v_hbm.at[:, columns(other)], i, other, reach_blocks + me)
        copy.start()
        v_copies.append(copy)

    pair = lax.broadcasted_iota(jnp.int32, (HD // 2, rows), 0)
    axis_of = 3 * pair // (HD // 2)
    load_coords.wait()
    position = jnp.where(
        axis_of == 0,
        coords_ref[0:1, :],
        jnp.where(axis_of == 1, coords_ref[1:2, :], coords_ref[2:3, :]),
    ).astype(jnp.float32)
    frequency = jnp.zeros((HD // 2, rows), jnp.float32)
    for p, value in enumerate(frequencies()):
        frequency = jnp.where(pair == p, value, frequency)
    angles = position * frequency

    def spread(table):
        tall = jnp.concatenate([table] * (128 // (HD // 2)), axis=0).T
        return jnp.concatenate([tall] * (cols // 128), axis=1)

    cos_all = spread(jnp.cos(angles))
    sin_all = spread(jnp.sin(angles))
    from_row = lax.broadcasted_iota(jnp.int32, (cols, cols), 0)
    to_col = lax.broadcasted_iota(jnp.int32, (cols, cols), 1)
    front = to_col % HD < HD // 2
    swap = jnp.where(
        front & (from_row == to_col + HD // 2),
        -1.0,
        jnp.where((to_col % HD >= HD // 2) & (from_row == to_col - HD // 2), 1.0, 0.0),
    ).astype(jnp.bfloat16)

    def rotated(tile, scale):
        swapped = jnp.dot(tile, swap, preferred_element_type=jnp.float32)
        turned = tile.astype(jnp.float32) * cos_all + swapped * sin_all
        return (turned * scale).astype(jnp.bfloat16)

    load_k.wait()
    k_copies = []
    for i in range(1, members):
        other = (me + i) % members
        k_rot[i] = rotated(k_in[:, columns(other)], 1.0).T
        copy = kv_copy(1, k_rot.at[i], i, other, reach_blocks + me)
        copy.start()
        k_copies.append(copy)
    k_buf[reach_blocks + me] = rotated(k_in[:, columns(me)], 1.0).T

    for e in shifts:
        held = [p for p in range(members) if 0 <= reach_blocks + p - e * members < blocks]
        low = reach_blocks + held[0] - e * members
        high = reach_blocks + held[-1] - e * members + 1

        @pl.when((group - e < 0) | (group - e >= groups))
        def _():
            for buf in bufs:
                buf[low:high] = jnp.zeros((high - low,) + buf.shape[1:], jnp.bfloat16)

    def halo_copy(which, p, e):
        index = reach_blocks + p - e * members
        return pltpu.make_async_remote_copy(
            src_ref=bufs[which].at[reach_blocks + p],
            dst_ref=bufs[which].at[index],
            send_sem=halo_send.at[which, shifts.index(e), p],
            recv_sem=kv_recv.at[which, index],
            device_id=device(group + e, me),
        )

    routes = [
        (p, [e for e in shifts if 0 <= reach_blocks + p - e * members < blocks])
        for p in range(members)
    ]
    routes.sort(key=lambda route: -len(route[1]))
    def pass_on(which):
        for p, goes in routes:

            @pl.when(me != p)
            def _():
                kv_copy(which, bufs[which].at[0], 0, p, reach_blocks + p).wait_recv()

            for e in goes:

                @pl.when((group + e >= 0) & (group + e < groups))
                def _():
                    halo_copy(which, p, e).start()

    own_v.wait()
    pass_on(0)

    load_q.wait()
    q_copies = []
    for i in range(1, members):
        other = (me + i) % members
        q_rot[i] = rotated(q_in[:, columns(other)], SCORE_SCALE)
        copy = pltpu.make_async_remote_copy(
            src_ref=q_rot.at[i],
            dst_ref=q_buf.at[block(me)],
            send_sem=q_send.at[i],
            recv_sem=q_recv.at[me],
            device_id=device(group, other),
        )
        copy.start()
        q_copies.append(copy)
    q_buf[block(me), :] = rotated(q_in[:, columns(me)], SCORE_SCALE)

    first = (group * members - reach_blocks) * rows
    token = first + lax.broadcasted_iota(jnp.int32, (8, blocks * rows), 1)
    scene = jnp.zeros((8, blocks * rows), jnp.int32)
    load_lengths.wait()
    end = jnp.int32(0)
    for s in range(scenes):
        end = end + lengths_ref[s]
        scene = scene + (token >= end).astype(jnp.int32)
    key_scene[...] = jnp.where(token < 0, -1, scene).astype(jnp.float32)
    for b in range(members):
        row = key_scene[0:1, (reach_blocks + b) * rows : (reach_blocks + b + 1) * rows]
        query_scene[b] = jnp.broadcast_to(row, (128, rows)).T

    pass_on(1)

    def halo_wait():
        for which in range(2):
            for p, goes in routes:
                for e in goes:

                    @pl.when((group - e >= 0) & (group - e < groups))
                    def _():
                        halo_copy(which, p, e).wait_recv()

    lane_head = lax.broadcasted_iota(jnp.int32, (rows, cols), 1) // HD

    own_o = pltpu.make_async_copy(o_buf.at[me], out_ref.at[:, columns(me)], own_sem.at[1])

    def out_copy(other):
        return pltpu.make_async_remote_copy(
            src_ref=o_buf.at[other],
            dst_ref=out_ref.at[:, columns(me)],
            send_sem=o_send.at[other],
            recv_sem=o_recv.at[me],
            device_id=device(group, other),
        )

    free = max(0, members - 2 * reach_blocks)

    def attend(t, carry):
        if isinstance(t, int):
            b = reach_blocks + (me + t) % free
        else:
            turn = (me + t) % (members - free)
            b = turn + free * (turn // reach_blocks)

        @pl.when(b != me)
        def _():
            pltpu.make_async_remote_copy(
                src_ref=q_rot.at[0],
                dst_ref=q_buf.at[block(b)],
                send_sem=q_send.at[0],
                recv_sem=q_recv.at[b],
                device_id=device(group, b),
            ).wait_recv()

        q_tile = q_buf[block(b), :]
        span = pl.ds(pl.multiple_of(b * rows, rows), window)
        count = window // rows
        k_tile = jnp.concatenate([k_buf[b + c] for c in range(count)], axis=1)
        v_tile = v_buf[pl.ds(b, count)].reshape(window, cols)
        q_scene = jnp.concatenate([query_scene[b]] * (window // 128), axis=1)
        bias = jnp.where(q_scene == key_scene[0:1, span], 0.0, NEG_BIG)
        result = jnp.zeros((rows, cols), jnp.float32)
        for h in range(heads):
            q_one = jnp.where(lane_head == h, q_tile, jnp.bfloat16(0.0))
            scores = jnp.dot(q_one, k_tile, preferred_element_type=jnp.float32) + bias
            top = jnp.max(scores, axis=1, keepdims=True)
            weights = jnp.exp(scores - top)
            total = jnp.sum(weights, axis=1, keepdims=True)
            mixed = jnp.dot(
                weights.astype(jnp.bfloat16), v_tile, preferred_element_type=jnp.float32
            )
            result = jnp.where(lane_head == h, mixed / total, result)
        o_buf[b] = result.astype(jnp.bfloat16)

        @pl.when(b != me)
        def _():
            out_copy(b).start()

        @pl.when(b == me)
        def _():
            own_o.start()

        return carry

    for t in range(free):
        attend(t, 0)
    halo_wait()
    lax.fori_loop(0, members - free, attend, 0)

    for copy in v_copies + k_copies + q_copies:
        copy.wait_send()
    for which in range(2):
        for p, goes in routes:
            for e in goes:

                @pl.when((group + e >= 0) & (group + e < groups))
                def _():
                    halo_copy(which, p, e).wait_send()

    for i in range(1, members):
        out_copy((me + i) % members).wait_send()
    for i in range(1, members):
        other = (me + i) % members
        pltpu.make_async_remote_copy(
            src_ref=o_buf.at[0],
            dst_ref=out_ref.at[:, columns(other)],
            send_sem=o_send.at[0],
            recv_sem=o_recv.at[other],
            device_id=device(group, other),
        ).wait_recv()
    own_o.wait()


def local(queries, keys, values, coords, lengths):
    rows, all_cols = queries.shape
    head_count = lax.axis_size("head")
    seq_count = lax.axis_size("seq")
    members = GROUP_DEVICES
    groups = seq_count * head_count // members
    cols = all_cols // members
    scenes = lengths.shape[0]
    total = rows * seq_count * head_count
    longest = 3 * total // scenes
    reach_blocks = -(-(longest - 1) // rows)
    blocks = members + 2 * reach_blocks
    spans = -(-reach_blocks // members)
    sizes = (head_count, members, groups, rows, cols, reach_blocks, scenes)
    window = (2 * reach_blocks + 1) * rows
    bf16, dma = jnp.bfloat16, pltpu.SemaphoreType.DMA
    in_hbm = pl.BlockSpec(memory_space=pltpu.HBM)
    return pl.pallas_call(
        functools.partial(attention_kernel, sizes),
        out_shape=jax.ShapeDtypeStruct((rows, all_cols), bf16),
        in_specs=[in_hbm] * 5,
        out_specs=in_hbm,
        scratch_shapes=[
            pltpu.VMEM(coords.shape, jnp.int32),
            pltpu.SMEM(lengths.shape, jnp.int32),
            pltpu.VMEM((rows, all_cols), bf16),
            pltpu.VMEM((rows, all_cols), bf16),
            pltpu.VMEM((members, rows, cols), bf16),
            pltpu.VMEM((members, cols, rows), bf16),
            pltpu.VMEM((members * rows, cols), bf16),
            pltpu.VMEM((blocks, cols, rows), bf16),
            pltpu.VMEM((blocks, rows, cols), bf16),
            pltpu.VMEM((members, rows, cols), bf16),
            pltpu.VMEM((8, blocks * rows), jnp.float32),
            pltpu.VMEM((members, rows, 128), jnp.float32),
            dma((4,)),
            dma((members,)),
            dma((members,)),
            dma((2, members)),
            dma((2, blocks)),
            dma((2, 2 * spans, members)),
            dma((members,)),
            dma((members,)),
            dma((2,)),
        ],
        compiler_params=pltpu.CompilerParams(
            collective_id=0, has_side_effects=True, vmem_limit_bytes=63 * 1024 * 1024
        ),
        cost_estimate=pl.CostEstimate(
            flops=4 * members * rows * window * cols,
            bytes_accessed=8 * rows * all_cols,
            transcendentals=members * rows * window * (cols // HD),
        ),
    )(queries, keys, values, coords, lengths)


def solution(mesh):
    in_specs = (
        P(("dp", "seq", "head"), None),
        P(("dp", "seq", "head"), None),
        P(("dp", "seq", "head"), None),
        P(None, ("dp", "seq", "head")),
        P("dp"),
    )
    out_specs = P(("dp", "seq", "head"), None)
    return jax.shard_map(local, mesh=mesh, in_specs=in_specs, out_specs=out_specs, check_vma=False)
```

```python
import functools

import jax
import jax.numpy as jnp
import numpy as np
from jax import lax
from jax.experimental import pallas as pl
from jax.experimental.pallas import tpu as pltpu
from jax.sharding import PartitionSpec as P

HD = 64
GROUP_DEVICES = 8
PARTS = 1
WAVES = 1
NEG_BIG = -1e30
SCORE_SCALE = 0.125


def frequencies():
    pair_count = HD // 2
    exponent = (3 * np.arange(pair_count) % pair_count) / pair_count
    return [float(f) for f in (100.0 ** -exponent).astype(np.float32)]


def attention_kernel(
    sizes,
    q_hbm, k_hbm, v_hbm, coords_hbm, lengths_hbm,
    out_ref,
    coords_ref, lengths_ref, q_in, k_in, q_rot, k_rot, q_buf, k_buf, v_buf, o_buf,
    key_scene, query_scene,
    in_sem, q_send, q_recv, kv_send, kv_recv, halo_send, o_send, o_recv, own_v_sem, own_o_sem,
):
    head_count, members, groups, rows, cols, parts, reach_blocks, scenes = sizes
    heads = cols // HD
    spans = -(-reach_blocks // members)
    blocks = members + 2 * reach_blocks
    count = 2 * reach_blocks + 1
    window = count * rows
    flat = lax.axis_index("seq") * head_count + lax.axis_index("head")
    group = flat // members
    me = flat % members

    def device(group_at, member_at):
        at = group_at * members + member_at
        return {"seq": at // head_count, "head": at % head_count}

    def columns(member_at, part):
        return pl.ds(pl.multiple_of((member_at * parts + part) * cols, cols), cols)

    shifts = [e for d in range(1, spans + 1) for e in (d, -d)]
    others = [(i, (me + i) % members) for i in range(1, members)]

    load_k = pltpu.make_async_copy(k_hbm, k_in, in_sem.at[0])
    load_q = pltpu.make_async_copy(q_hbm, q_in, in_sem.at[1])
    load_coords = pltpu.make_async_copy(coords_hbm, coords_ref, in_sem.at[2])
    load_lengths = pltpu.make_async_copy(lengths_hbm, lengths_ref, in_sem.at[3])
    load_coords.start()
    load_k.start()
    load_q.start()
    load_lengths.start()
    own_v = [
        pltpu.make_async_copy(
            v_hbm.at[:, columns(me, part)], v_buf.at[part, reach_blocks + me], own_v_sem.at[part]
        )
        for part in range(parts)
    ]
    for copy in own_v:
        copy.start()

    barrier = pltpu.get_barrier_semaphore()
    for i, other in others:
        pl.semaphore_signal(barrier, inc=1, device_id=device(group, other))
    expected = members - 1
    for e in shifts:
        there = (group + e >= 0) & (group + e < groups)

        @pl.when(there)
        def _():
            pl.semaphore_signal(barrier, inc=1, device_id=device(group + e, me))

        expected = expected + there.astype(jnp.int32)
    pl.semaphore_wait(barrier, expected)

    bufs = (v_buf, k_buf)

    def kv_copy(which, part, source, i, other, index):
        return pltpu.make_async_remote_copy(
            src_ref=source,
            dst_ref=bufs[which].at[part, index],
            send_sem=kv_send.at[which, part, i],
            recv_sem=kv_recv.at[which, part, index],
            device_id=device(group, other),
        )

    def v_copy(part, i, other):
        source = v_hbm.at[:, columns(other, part)]
        return kv_copy(0, part, source, i, other, reach_blocks + me)

    def k_copy(part, i, other):
        return kv_copy(1, part, k_rot.at[part, i], i, other, reach_blocks + me)

    wave_rows = rows // WAVES

    def q_copy(part, wave, i, other, at):
        cut = slice(wave * wave_rows, (wave + 1) * wave_rows)
        return pltpu.make_async_remote_copy(
            src_ref=q_rot.at[part, i, cut],
            dst_ref=q_buf.at[part, at, cut],
            send_sem=q_send.at[part, wave, i],
            recv_sem=q_recv.at[part, wave, at],
            device_id=device(group, other),
        )

    def start_v(part):
        for i, other in others:
            v_copy(part, i, other).start()

    start_v(0)

    pair = lax.broadcasted_iota(jnp.int32, (HD // 2, rows), 0)
    axis_of = 3 * pair // (HD // 2)
    load_coords.wait()
    position = jnp.where(
        axis_of == 0,
        coords_ref[0:1, :],
        jnp.where(axis_of == 1, coords_ref[1:2, :], coords_ref[2:3, :]),
    ).astype(jnp.float32)
    frequency = jnp.zeros((HD // 2, rows), jnp.float32)
    for p, value in enumerate(frequencies()):
        frequency = jnp.where(pair == p, value, frequency)
    angles = position * frequency

    def spread(table):
        return jnp.concatenate([table] * (cols // (HD // 2)), axis=0).T

    cos_all = spread(jnp.cos(angles))
    sin_all = spread(jnp.sin(angles))
    from_row = lax.broadcasted_iota(jnp.int32, (cols, cols), 0)
    to_col = lax.broadcasted_iota(jnp.int32, (cols, cols), 1)
    front = to_col % HD < HD // 2
    swap = jnp.where(
        front & (from_row == to_col + HD // 2),
        -1.0,
        jnp.where((to_col % HD >= HD // 2) & (from_row == to_col - HD // 2), 1.0, 0.0),
    ).astype(jnp.bfloat16)

    def rotated(tile, scale):
        swapped = jnp.dot(tile, swap, preferred_element_type=jnp.float32)
        turned = tile.astype(jnp.float32) * cos_all + swapped * sin_all
        return (turned * scale).astype(jnp.bfloat16)

    def rotate_k(part, send):
        for i, other in others:
            k_rot[part, i] = rotated(k_in[:, columns(other, part)], 1.0).T
            if send:
                k_copy(part, i, other).start()
        k_buf[part, reach_blocks + me] = rotated(k_in[:, columns(me, part)], 1.0).T

    def rotate_q(part, send):
        for i, other in others:
            q_rot[part, i] = rotated(q_in[:, columns(other, part)], SCORE_SCALE)
            if send:
                q_copy(part, 0, i, other, me).start()
        q_buf[part, me] = rotated(q_in[:, columns(me, part)], SCORE_SCALE)
        for wave in range(1, WAVES):
            for i, other in others:
                q_copy(part, wave, i, other, me).start()

    load_k.wait()
    rotate_k(0, True)
    load_q.wait()
    rotate_q(0, True)

    for e in shifts:
        held = [p for p in range(members) if 0 <= reach_blocks + p - e * members < blocks]
        low = reach_blocks + held[0] - e * members
        high = reach_blocks + held[-1] - e * members + 1

        @pl.when((group - e < 0) | (group - e >= groups))
        def _():
            for buf in bufs:
                for part in range(parts):
                    buf[part, low:high] = jnp.zeros((high - low,) + buf.shape[2:], jnp.bfloat16)

    def halo_copy(which, part, p, e):
        index = reach_blocks + p - e * members
        return pltpu.make_async_remote_copy(
            src_ref=bufs[which].at[part, reach_blocks + p],
            dst_ref=bufs[which].at[part, index],
            send_sem=halo_send.at[which, part, shifts.index(e), p],
            recv_sem=kv_recv.at[which, part, index],
            device_id=device(group + e, me),
        )

    routes = [
        (p, [e for e in shifts if 0 <= reach_blocks + p - e * members < blocks])
        for p in range(members)
    ]
    routes.sort(key=lambda route: -len(route[1]))

    def pass_on(which, part):
        for p, goes in routes:

            @pl.when(me != p)
            def _():
                kv_copy(which, part, bufs[which].at[part, 0], 0, p, reach_blocks + p).wait_recv()

            for e in goes:

                @pl.when((group + e >= 0) & (group + e < groups))
                def _():
                    halo_copy(which, part, p, e).start()

    def halo_wait(part):
        for which in range(2):
            for p, goes in routes:
                for e in goes:

                    @pl.when((group - e >= 0) & (group - e < groups))
                    def _():
                        halo_copy(which, part, p, e).wait_recv()

    lane_head = lax.broadcasted_iota(jnp.int32, (wave_rows, cols), 1) // HD

    def own_o(part):
        return pltpu.make_async_copy(
            o_buf.at[part, me], out_ref.at[:, columns(me, part)], own_o_sem.at[part]
        )

    def out_copy(part, wave, other, writer):
        cut = slice(wave * wave_rows, (wave + 1) * wave_rows)
        return pltpu.make_async_remote_copy(
            src_ref=o_buf.at[part, other, cut],
            dst_ref=out_ref.at[cut, columns(writer, part)],
            send_sem=o_send.at[part, wave, other],
            recv_sem=o_recv.at[part, wave, writer],
            device_id=device(group, other),
        )

    free = max(0, members - 2 * reach_blocks)

    def mixed_rows(part, wave, b):
        cut = slice(wave * wave_rows, (wave + 1) * wave_rows)
        q_tile = q_buf[part, b, cut]
        span = pl.ds(pl.multiple_of(b * rows, rows), window)
        k_tile = jnp.concatenate([k_buf[part, b + c] for c in range(count)], axis=1)
        v_tile = v_buf[part, pl.ds(b, count)].reshape(window, cols)
        q_scene = jnp.concatenate([query_scene[b, cut]] * (window // 128), axis=1)
        bias = jnp.where(q_scene == key_scene[0:1, span], 0.0, NEG_BIG)
        result = jnp.zeros((wave_rows, cols), jnp.float32)
        for h in range(heads):
            q_one = jnp.where(lane_head == h, q_tile, jnp.bfloat16(0.0))
            scores = jnp.dot(q_one, k_tile, preferred_element_type=jnp.float32) + bias
            top = jnp.max(scores, axis=1, keepdims=True)
            weights = jnp.exp(scores - top)
            total = jnp.sum(weights, axis=1, keepdims=True)
            mixed = jnp.dot(
                weights.astype(jnp.bfloat16), v_tile, preferred_element_type=jnp.float32
            )
            result = jnp.where(lane_head == h, mixed / total, result)
        return result.astype(jnp.bfloat16)

    def attend(part, wave, picked):
        cut = slice(wave * wave_rows, (wave + 1) * wave_rows)
        for b in picked:

            @pl.when(b != me)
            def _():
                q_copy(part, wave, 0, b, b).wait_recv()

        results = [mixed_rows(part, wave, b) for b in picked]
        for b, result in zip(picked, results):
            o_buf[part, b, cut] = result
        for b in picked:

            @pl.when(b != me)
            def _():
                out_copy(part, wave, b, me).start()

    def later(t):
        turn = (me + t) % (members - free)
        return turn + free * (turn // reach_blocks)

    def attend_all(part):
        for wave in range(WAVES):
            for t in range(0, free, 2):
                attend(part, wave, [reach_blocks + (me + t + u) % free for u in range(2)])
            if wave == 0:
                halo_wait(part)

            @pl.loop(0, (members - free) // 2)
            def _(t):
                attend(part, wave, [later(2 * t), later(2 * t + 1)])

        own_o(part).start()

    own_v[0].wait()
    pass_on(0, 0)
    for part in range(1, parts):
        start_v(part)
        rotate_k(part, True)

    first = (group * members - reach_blocks) * rows
    token = first + lax.broadcasted_iota(jnp.int32, (8, blocks * rows), 1)
    scene = jnp.zeros((8, blocks * rows), jnp.int32)
    load_lengths.wait()
    end = jnp.int32(0)
    for s in range(scenes):
        end = end + lengths_ref[s]
        scene = scene + (token >= end).astype(jnp.int32)
    key_scene[...] = jnp.where(token < 0, -1, scene).astype(jnp.float32)
    for b in range(members):
        row = key_scene[0:1, (reach_blocks + b) * rows : (reach_blocks + b + 1) * rows]
        query_scene[b] = jnp.broadcast_to(row, (128, rows)).T

    pass_on(1, 0)
    for part in range(1, parts):
        rotate_q(part, True)

    for part in range(parts):
        if part:
            own_v[part].wait()
            pass_on(0, part)
            pass_on(1, part)
        attend_all(part)

    for part in range(parts):
        for i, other in others:
            v_copy(part, i, other).wait_send()
            k_copy(part, i, other).wait_send()
            for wave in range(WAVES):
                q_copy(part, wave, i, other, me).wait_send()
        for which in range(2):
            for p, goes in routes:
                for e in goes:

                    @pl.when((group + e >= 0) & (group + e < groups))
                    def _():
                        halo_copy(which, part, p, e).wait_send()

        for wave in range(WAVES):
            for i, other in others:
                out_copy(part, wave, other, me).wait_send()
            for i, other in others:
                out_copy(part, wave, other, other).wait_recv()
        own_o(part).wait()


def local(queries, keys, values, coords, lengths):
    rows, all_cols = queries.shape
    head_count = lax.axis_size("head")
    seq_count = lax.axis_size("seq")
    members = GROUP_DEVICES
    groups = seq_count * head_count // members
    parts = PARTS
    cols = all_cols // members // parts
    scenes = lengths.shape[0]
    total = rows * seq_count * head_count
    longest = 3 * total // scenes
    reach_blocks = -(-(longest - 1) // rows)
    blocks = members + 2 * reach_blocks
    spans = -(-reach_blocks // members)
    sizes = (head_count, members, groups, rows, cols, parts, reach_blocks, scenes)
    window = (2 * reach_blocks + 1) * rows
    bf16, dma = jnp.bfloat16, pltpu.SemaphoreType.DMA
    in_hbm = pl.BlockSpec(memory_space=pltpu.HBM)
    return pl.pallas_call(
        functools.partial(attention_kernel, sizes),
        out_shape=jax.ShapeDtypeStruct((rows, all_cols), bf16),
        in_specs=[in_hbm] * 5,
        out_specs=in_hbm,
        scratch_shapes=[
            pltpu.VMEM(coords.shape, jnp.int32),
            pltpu.SMEM(lengths.shape, jnp.int32),
            pltpu.VMEM((rows, all_cols), bf16),
            pltpu.VMEM((rows, all_cols), bf16),
            pltpu.VMEM((parts, members, rows, cols), bf16),
            pltpu.VMEM((parts, members, cols, rows), bf16),
            pltpu.VMEM((parts, members, rows, cols), bf16),
            pltpu.VMEM((parts, blocks, cols, rows), bf16),
            pltpu.VMEM((parts, blocks, rows, cols), bf16),
            pltpu.VMEM((parts, members, rows, cols), bf16),
            pltpu.VMEM((8, blocks * rows), jnp.float32),
            pltpu.VMEM((members, rows, 128), jnp.float32),
            dma((4,)),
            dma((parts, WAVES, members)),
            dma((parts, WAVES, members)),
            dma((2, parts, members)),
            dma((2, parts, blocks)),
            dma((2, parts, 2 * spans, members)),
            dma((parts, WAVES, members)),
            dma((parts, WAVES, members)),
            dma((parts,)),
            dma((parts,)),
        ],
        compiler_params=pltpu.CompilerParams(
            collective_id=0, has_side_effects=True, vmem_limit_bytes=63 * 1024 * 1024
        ),
        cost_estimate=pl.CostEstimate(
            flops=4 * members * rows * window * cols * parts,
            bytes_accessed=8 * rows * all_cols,
            transcendentals=members * rows * window * (cols // HD) * parts,
        ),
    )(queries, keys, values, coords, lengths)


def solution(mesh):
    in_specs = (
        P(("dp", "seq", "head"), None),
        P(("dp", "seq", "head"), None),
        P(("dp", "seq", "head"), None),
        P(None, ("dp", "seq", "head")),
        P("dp"),
    )
    out_specs = P(("dp", "seq", "head"), None)
    return jax.shard_map(local, mesh=mesh, in_specs=in_specs, out_specs=out_specs, check_vma=False)
```
